32 devices in a mesh: gx: 8 (over z, x), ma: 4 (over y, core).
Axes of the slice: x: 2, y: 2, z: 4, core: 2. Of those that a mesh axis runs over, the one named last changes fastest.
Arguments:
- solution: float32 [256, 8, 8, 256], P('ma', 'gx'), may hold values from -1.2 to 1.2
- source: float32 [256, 8, 8, 256], P('ma', 'gx'), may hold values from -6 to 6
- mean_conductivity: float32 [8, 8, 256], P('gx'), may hold values from 0.5 to 2
- kl_fields: float32 [10, 8, 8, 256], P(None, 'gx'), may hold values from -0.9 to 0.9
- couplings: int32 [10, 256, 2], replicated, may hold values from 0 to 255, as said below
- mode_index: int32 [256, 10], replicated, may hold values from 0 to 3, as said below
Outputs:
- residual: float32 [256, 8, 8, 256], P('ma', 'gx')
- correction: float32 [256, 8, 8, 256], P('ma', 'gx')
The draws below stay inside these ranges and needn't reach their ends.
Inputs may be any that keep to these rules, and one draw needn't show every extreme that they name: couplings[k, i, 0] is the mode whose multi-index is mode_index[i] plus one in variable k, couplings[k, i, 1] the mode whose multi-index is mode_index[i] minus one in variable k; where no mode has that multi-index the entry is i itself. `mode_index`: the rows are 256 distinct multi-indices of total degree at most 3 in graded order: the total degree never falls with the mode number, all multi-indices of each total degree below 3 are present, and some mode has degree 3 in one variable; the order of the variables is drawn from the seed.
All inputs are finite; a program needn't handle non-finite values.
Results may differ from the reference program's by a relative error of at most 0.000071.
Values sent between devices are 32-bit elements; how exact they have to be, the bound alone decides.
A program may use at most 128 MiB of HBM per device.

```python
import jax
import jax.numpy as jnp
import numpy as np
from jax import lax

NY = 8
NZ = 256
P_SIZE = 256
KL = 10
DEG = 3
S = 2
STEPS = 3
NX = 8


def basis_table():
    entries = [[]]
    for variable in range(KL):
        extended = []
        for entry in entries:
            for levels in range(DEG - sum(entry) + 1):
                extended.append(entry + [levels])
        entries = extended
    entries.sort(key=lambda entry: (sum(entry), [-level_value for level_value in entry]))
    return np.array(entries[:P_SIZE], dtype=np.int32)


def chaos_tables(key):
    basis = jnp.asarray(basis_table())
    variable_order = jax.random.permutation(jax.random.fold_in(key, 7), KL)
    indices = jnp.take(basis, variable_order, axis=1).astype(jnp.int32)
    unit_steps = jnp.eye(KL, dtype=jnp.int32)
    mode_ids = jnp.arange(P_SIZE, dtype=jnp.int32)
    partners = []
    for shifted in (1, -1):
        target = indices[None, :, :] + shifted * unit_steps[:, None, :]
        matches = jnp.all(target[:, :, None, :] == indices[None, None, :, :], axis=-1)
        present = jnp.any(matches, axis=-1)
        located = jnp.sum(matches.astype(jnp.int32) * mode_ids[None, None, :], axis=-1)
        partners.append(jnp.where(present, located, jnp.broadcast_to(mode_ids[None, :], located.shape)))
    return (indices, jnp.stack(partners, -1).astype(jnp.int32))


def draw_couplings(key, part):
    return chaos_tables(key)[1]


def draw_mode_index(key, part):
    return chaos_tables(key)[0]


def steps_of(rng, shape, cuts, least, high):
    def one(dim, parts):
        steps = jax.random.uniform(jax.random.fold_in(jax.random.fold_in(rng, 6), dim), (parts,), jnp.float32, least / len(cuts), high / len(cuts))
        return jnp.repeat(jnp.exp(steps), shape[dim] // parts).reshape((-1,) + (1,) * (len(shape) - dim - 1))

    loudness = one(*cuts[0])
    for cut in cuts[1:]:
        loudness = loudness * one(*cut)
    return loudness


def bell_draw(key, shape, spread, bound, shards=(), kind=jnp.bfloat16):
    drawn = jax.random.normal(key, shape, jnp.float32) * spread
    if len(shards) > 0:
        drawn = steps_of(key, shape, shards, -0.22, 0.18) * drawn
    return jnp.clip(drawn, min=-bound, max=bound).astype(kind)


def setup_inputs(seed: int = 0) -> dict:
    arg_keys = jax.random.split(jax.random.key(seed), 7)
    return {
        "solution": bell_draw(arg_keys[0], (P_SIZE, NX, NY, NZ), 0.2, 1.2, ((0, 4), (1, 8)), jnp.float32),
        "source": bell_draw(arg_keys[1], (P_SIZE, NX, NY, NZ), 1.0, 6.0, ((0, 4), (1, 8)), jnp.float32),
        "mean_conductivity": jnp.clip(0.5 + 1.5 * jax.random.uniform(arg_keys[2], (NX, NY, NZ), jnp.float32) ** steps_of(arg_keys[2], (NX, NY, NZ), ((0, 8),), -0.2, 0.2), 0.5, 2.0),
        "kl_fields": bell_draw(arg_keys[3], (KL, NX, NY, NZ), 0.15, 0.9, ((1, 8),), jnp.float32),
        "couplings": draw_couplings(jax.random.fold_in(arg_keys[6], 71), 0),
        "mode_index": draw_mode_index(jax.random.fold_in(arg_keys[6], 71), 0),
    }


def periodic_pad(values, which_dim):
    length = values.shape[which_dim]
    last = lax.slice_in_dim(values, length - 1, length, axis=which_dim)
    first = lax.slice_in_dim(values, 0, 1, axis=which_dim)
    return jnp.concatenate([last, values, first], axis=which_dim)

def diffuse(coefficient, padded):
    center = coefficient[1:-1]
    values = padded[..., 1:-1, :, :]
    total = 0.5 * (center + coefficient[2:]) * (values - padded[..., 2:, :, :])
    total = total + 0.5 * (center + coefficient[:-2]) * (values - padded[..., :-2, :, :])
    for which_dim in (-2, -1):
        for offset in (-1, 1):
            total = total + 0.5 * (center + jnp.roll(center, offset, which_dim)) * (values - jnp.roll(values, offset, which_dim))
    return total

def reference(solution, source, mean_conductivity, kl_fields, couplings, mode_index):
    padded_solution = periodic_pad(solution, 1)
    mean_pad = periodic_pad(mean_conductivity, 0)
    kl_pad = periodic_pad(kl_fields, 1)
    mode_ids = jnp.arange(P_SIZE, dtype=jnp.int32)
    image = solution + diffuse(mean_pad, padded_solution)
    for field_id in range(KL):
        applied = diffuse(kl_pad[field_id], padded_solution)
        partners = couplings[field_id]
        degree = mode_index[:, field_id]
        for second in range(S):
            column = partners[:, second]
            strength = jnp.sqrt(jnp.maximum(degree, degree[column]).astype(jnp.float32))
            weight = jnp.where(column != mode_ids, strength, jnp.zeros_like(strength))
            image = image + weight[:, None, None, None] * applied[column]
    residual = source - image
    theta = 13.0
    delta = 12.0
    sigma = theta / delta
    rho = 1.0 / sigma
    direction = residual / theta
    correction = direction
    remain = residual
    for step in range(STEPS):
        applied = direction + diffuse(mean_pad, periodic_pad(direction, 1))
        remain = remain - applied
        rho_next = 1.0 / (2.0 * sigma - rho)
        direction = rho_next * rho * direction + 2.0 * rho_next / delta * remain
        correction = correction + direction
        rho = rho_next
    return (residual, correction)
```

```python
import functools

import jax
import jax.numpy as jnp
from jax import lax
from jax.experimental import pallas as pl
from jax.experimental.pallas import tpu as pltpu
from jax.sharding import PartitionSpec as P

STEPS = 3
MESH = pl.DeviceIdType.MESH
VMEM = pl.BlockSpec(memory_space=pltpu.VMEM)
SMEM = pl.BlockSpec(memory_space=pltpu.SMEM)
LIMIT = 40 * 1024 * 1024


def greet(gx, n_gx, ma, n_ma):
    barrier = pltpu.get_barrier_semaphore()
    for d in range(1, n_gx):
        pl.semaphore_signal(barrier, inc=1, device_id={"gx": lax.rem(gx + d, n_gx)}, device_id_type=MESH)
    for d in range(1, n_ma):
        pl.semaphore_signal(barrier, inc=1, device_id={"ma": lax.rem(ma + d, n_ma)}, device_id_type=MESH)
    pl.semaphore_wait(barrier, max(n_gx - 1, 0) + max(n_ma - 1, 0))


def remote(src, dst, send, recv, axis, index):
    copy = pltpu.make_async_remote_copy(
        src_ref=src, dst_ref=dst, send_sem=send, recv_sem=recv, device_id={axis: index}, device_id_type=MESH
    )
    copy.start()
    return copy


def gather_kernel(n_gx, n_ma, v_ref, c_ref, all_ref, side_ref, mean_ref, s_v, r_v, s_c, r_c, s_m, r_m):
    gx, ma = lax.axis_index("gx"), lax.axis_index("ma")
    modes = v_ref.shape[0]
    greet(gx, n_gx, ma, n_ma)
    mine = pl.ds(ma * modes, modes)
    copies = []
    for d in range(n_ma - 1, 0, -1):
        copies.append(
            remote(v_ref, all_ref.at[mine], s_v.at[d], r_v.at[d], "ma", lax.rem(ma + d, n_ma))
        )
    copies.append(remote(c_ref, side_ref.at[1], s_c.at[1], r_c.at[1], "gx", lax.rem(gx + 1, n_gx)))
    copies.append(remote(c_ref, side_ref.at[0], s_c.at[0], r_c.at[0], "gx", lax.rem(gx + n_gx - 1, n_gx)))
    for d in range(1, n_gx):
        copies.append(
            remote(c_ref.at[0], mean_ref.at[gx], s_m.at[d], r_m.at[d], "gx", lax.rem(gx + d, n_gx))
        )
    all_ref[mine] = v_ref[...]
    mean_ref[gx] = c_ref[0]
    for copy in copies:
        copy.wait()


def faces_of(c):
    ny, nz = c.shape[-2], c.shape[-1]
    return [
        0.5 * (c + pltpu.roll(c, ny - 1, c.ndim - 2)),
        0.5 * (c + pltpu.roll(c, 1, c.ndim - 2)),
        0.5 * (c + pltpu.roll(c, nz - 1, c.ndim - 1)),
        0.5 * (c + pltpu.roll(c, 1, c.ndim - 1)),
    ]


def shift_faces(q):
    ny, nz = q[0].shape[-2], q[0].shape[-1]
    d = q[0].ndim
    return (
        pltpu.roll(q[1], ny - 1, d - 2)
        + pltpu.roll(q[0], 1, d - 2)
        + pltpu.roll(q[3], nz - 1, d - 1)
        + pltpu.roll(q[2], 1, d - 1)
    )


def couple_kernel(group, start_ref, part_ref, wt_ref, all_ref, src_ref, c_ref, side_ref, u_ref, qr_ref, ql_ref, f_ref):
    fields = c_ref.shape[0]
    modes = src_ref.shape[0]
    start = start_ref[0]
    for k in range(fields):
        c = c_ref[k]
        for m, face in enumerate(faces_of(c)):
            f_ref[m, k] = face
        f_ref[4, k] = 0.5 * (c + side_ref[0, k])
        f_ref[5, k] = 0.5 * (c + side_ref[1, k])

    def body(step, carry):
        base = step * group
        values = [all_ref[start + base + g] for g in range(group)]
        f = [f_ref[m, 0] for m in range(6)]
        q = [[f[m] * values[g] for m in range(6)] for g in range(group)]
        for k in range(1, fields):
            row = 2 * (k - 1)
            f = [f_ref[m, k] for m in range(6)]
            for g in range(group):
                i = base + g
                h = wt_ref[row, i] * all_ref[part_ref[row, i]] + wt_ref[row + 1, i] * all_ref[part_ref[row + 1, i]]
                q[g] = [q[g][m] + f[m] * h for m in range(6)]
        for g in range(group):
            total = q[g][0] + q[g][1] + q[g][2] + q[g][3] + q[g][4] + q[g][5]
            image = values[g] + total - shift_faces(q[g])
            u_ref[base + g] = src_ref[base + g] - image
            qr_ref[base + g] = q[g][4]
            ql_ref[base + g] = q[g][5]
        return carry

    lax.fori_loop(0, modes // group, body, 0)


def chebyshev_kernel(
    n_gx, u_ref, qr_ref, ql_ref, mean_ref, res_ref, cor_ref,
    from_left, from_right, trans, back, f_ref, s_r, r_r, s_l, r_l, s_t, r_t, s_b, r_b,
):
    gx = lax.axis_index("gx")
    modes = u_ref.shape[0]
    part = modes // n_gx
    right, left = lax.rem(gx + 1, n_gx), lax.rem(gx + n_gx - 1, n_gx)
    greet(gx, n_gx, 0, 1)
    order = list(range(1, n_gx)) + [0]
    halos = []
    for d in order:
        rows = pl.ds(d * part, part)
        halos.append(
            (
                remote(qr_ref.at[rows], from_left.at[rows], s_r.at[d], r_r.at[d], "gx", right),
                remote(ql_ref.at[rows], from_right.at[rows], s_l.at[d], r_l.at[d], "gx", left),
            )
        )
    for s in range(n_gx):
        c = mean_ref[s]
        after = mean_ref[(s + 1) % n_gx]
        before = mean_ref[(s + n_gx - 1) % n_gx]
        f = faces_of(c) + [0.5 * (c + after), 0.5 * (c + before)]
        for m in range(6):
            f_ref[m, s] = f[m]
        f_ref[6, s] = f[0] + f[1] + f[2] + f[3] + f[4] + f[5] + 1.0
    sent = []
    for d, pair in zip(order, halos):
        rows = pl.ds(d * part, part)
        pair[0].wait()
        pair[1].wait()
        res_ref[rows] = u_ref[rows] + from_left[rows] + from_right[rows]
    for d in range(n_gx):
        target = lax.rem(gx + d, n_gx)
        rows = pl.ds(target * part, part)
        if d == 0:
            trans[gx] = res_ref[rows]
        else:
            sent.append(
                remote(res_ref.at[rows], trans.at[gx], s_t.at[d], r_t.at[d], "gx", target)
            )
    for copy in sent:
        copy.wait()

    theta = 13.0
    delta = 12.0
    sigma = theta / delta

    def one(mode, carry):
        remain = [trans[s, mode] for s in range(n_gx)]
        direction = [r * (1.0 / theta) for r in remain]
        total = direction
        rho = 1.0 / sigma
        for _ in range(STEPS):
            rho_next = 1.0 / (2.0 * sigma - rho)
            ny, nz = direction[0].shape
            fresh = []
            for s in range(n_gx):
                v = direction[s]
                applied = (
                    f_ref[6, s] * v
                    - f_ref[0, s] * pltpu.roll(v, ny - 1, 0)
                    - f_ref[1, s] * pltpu.roll(v, 1, 0)
                    - f_ref[2, s] * pltpu.roll(v, nz - 1, 1)
                    - f_ref[3, s] * pltpu.roll(v, 1, 1)
                    - f_ref[4, s] * direction[(s + 1) % n_gx]
                    - f_ref[5, s] * direction[(s + n_gx - 1) % n_gx]
                )
                fresh.append(remain[s] - applied)
            remain = fresh
            direction = [
                (rho_next * rho) * direction[s] + (2.0 * rho_next / delta) * remain[s] for s in range(n_gx)
            ]
            total = [total[s] + direction[s] for s in range(n_gx)]
            rho = rho_next
        for s in range(n_gx):
            back[s, mode] = total[s]
        return carry

    lax.fori_loop(0, part, one, 0)
    sent = []
    for d in range(n_gx):
        target = lax.rem(gx + d, n_gx)
        rows = pl.ds(gx * part, part)
        if d == 0:
            cor_ref[rows] = back[gx]
        else:
            sent.append(
                remote(back.at[target], cor_ref.at[rows], s_b.at[d], r_b.at[d], "gx", target)
            )
    for copy in sent:
        copy.wait()


def shards(n_gx, n_ma, solution, source, mean_conductivity, kl_fields, couplings, mode_index):
    modes = solution.shape[0]
    shape = solution.shape
    ny, nz = shape[2], shape[3]
    fields = kl_fields.shape[0]
    start = lax.axis_index("ma") * modes
    f32 = jnp.float32
    here = lax.dynamic_slice_in_dim(couplings, start, modes, 1)
    degree = lax.dynamic_slice_in_dim(mode_index, start, modes, 0).T.astype(f32)
    ids = start + lax.broadcasted_iota(jnp.int32, (1, modes, 1), 1)
    strength = jnp.sqrt(jnp.stack([degree + 1.0, degree], -1))
    weight = jnp.where(here != ids, strength, 0.0)
    partner = here.transpose(0, 2, 1).reshape(2 * fields, modes)
    weight = weight.transpose(0, 2, 1).reshape(2 * fields, modes)
    stacked = jnp.concatenate([mean_conductivity, kl_fields[:, 0]], 0)
    v = solution.reshape(modes, ny, nz)
    src = source.reshape(modes, ny, nz)
    dma = pltpu.SemaphoreType.DMA
    everything, sides, means = pl.pallas_call(
        functools.partial(gather_kernel, n_gx, n_ma),
        out_shape=(
            jax.ShapeDtypeStruct((n_ma * modes, ny, nz), f32),
            jax.ShapeDtypeStruct((2, fields + 1, ny, nz), f32),
            jax.ShapeDtypeStruct((n_gx, ny, nz), f32),
        ),
        in_specs=[VMEM] * 2,
        out_specs=(VMEM,) * 3,
        scratch_shapes=[dma((n_ma,)), dma((n_ma,)), dma((2,)), dma((2,)), dma((n_gx,)), dma((n_gx,))],
        compiler_params=pltpu.CompilerParams(collective_id=0, has_side_effects=True, vmem_limit_bytes=LIMIT),
    )(v, stacked)
    field = jax.ShapeDtypeStruct((modes, ny, nz), f32)
    group = 2 if modes % 2 == 0 else 1
    u, qr, ql = pl.pallas_call(
        functools.partial(couple_kernel, group),
        out_shape=(field,) * 3,
        in_specs=[SMEM] * 3 + [VMEM] * 4,
        out_specs=(VMEM,) * 3,
        scratch_shapes=[pltpu.VMEM((6, fields + 1, ny, nz), f32)],
        compiler_params=pltpu.CompilerParams(vmem_limit_bytes=LIMIT),
    )(start.reshape(1).astype(jnp.int32), partner, weight, everything, src, stacked, sides)
    part = modes // n_gx
    residual, correction = pl.pallas_call(
        functools.partial(chebyshev_kernel, n_gx),
        out_shape=(field,) * 2,
        in_specs=[VMEM] * 4,
        out_specs=(VMEM,) * 2,
        scratch_shapes=[
            pltpu.VMEM((modes, ny, nz), f32),
            pltpu.VMEM((modes, ny, nz), f32),
            pltpu.VMEM((n_gx, part, ny, nz), f32),
            pltpu.VMEM((n_gx, part, ny, nz), f32),
            pltpu.VMEM((7, n_gx, ny, nz), f32),
        ]
        + [dma((n_gx,))] * 8,
        compiler_params=pltpu.CompilerParams(collective_id=1, has_side_effects=True, vmem_limit_bytes=LIMIT),
    )(u, qr, ql, means)
    return residual.reshape(shape), correction.reshape(shape)


def solution(mesh):
    in_specs = (
        P("ma", "gx", None, None),
        P("ma", "gx", None, None),
        P("gx", None, None),
        P(None, "gx", None, None),
        P(),
        P(),
    )
    out_specs = (P("ma", "gx", None, None), P("ma", "gx", None, None))
    body = functools.partial(shards, mesh.shape["gx"], mesh.shape["ma"])
    return jax.shard_map(body, mesh=mesh, in_specs=in_specs, out_specs=out_specs, check_vma=False)
```

```python
import functools

import jax
import jax.numpy as jnp
from jax import lax
from jax.experimental import pallas as pl
from jax.experimental.pallas import tpu as pltpu
from jax.sharding import PartitionSpec as P

STEPS = 3
MESH = pl.DeviceIdType.MESH
VMEM = pl.BlockSpec(memory_space=pltpu.VMEM)
SMEM = pl.BlockSpec(memory_space=pltpu.SMEM)
LIMIT = 40 * 1024 * 1024


def greet(gx, n_gx, ma, n_ma):
    barrier = pltpu.get_barrier_semaphore()
    for d in range(1, n_gx):
        pl.semaphore_signal(barrier, inc=1, device_id={"gx": lax.rem(gx + d, n_gx)}, device_id_type=MESH)
    for d in range(1, n_ma):
        pl.semaphore_signal(barrier, inc=1, device_id={"ma": lax.rem(ma + d, n_ma)}, device_id_type=MESH)
    pl.semaphore_wait(barrier, max(n_gx - 1, 0) + max(n_ma - 1, 0))


def remote(src, dst, send, recv, axis, index):
    copy = pltpu.make_async_remote_copy(
        src_ref=src, dst_ref=dst, send_sem=send, recv_sem=recv, device_id={axis: index}, device_id_type=MESH
    )
    copy.start()
    return copy


def faces_of(c):
    ny, nz = c.shape[-2], c.shape[-1]
    return [
        0.5 * (c + pltpu.roll(c, ny - 1, c.ndim - 2)),
        0.5 * (c + pltpu.roll(c, 1, c.ndim - 2)),
        0.5 * (c + pltpu.roll(c, nz - 1, c.ndim - 1)),
        0.5 * (c + pltpu.roll(c, 1, c.ndim - 1)),
    ]


def shift_faces(q):
    ny, nz = q[0].shape[-2], q[0].shape[-1]
    d = q[0].ndim
    return (
        pltpu.roll(q[1], ny - 1, d - 2)
        + pltpu.roll(q[0], 1, d - 2)
        + pltpu.roll(q[3], nz - 1, d - 1)
        + pltpu.roll(q[2], 1, d - 1)
    )


def kernel(
    n_gx, n_ma, chunks, pieces, part_ref, wt_ref, v_ref, src_ref, c_ref, res_ref, cor_ref,
    all_ref, side_ref, mean_ref, f_ref, fm_ref, u_ref, qr_ref, ql_ref, from_left, from_right, trans, back,
    s_p, r_p, s_f, r_f, s_o, r_o, s_c, r_c, s_m, r_m, s_h, r_h, s_t, r_t, s_b, r_b,
):
    gx, ma = lax.axis_index("gx"), lax.axis_index("ma")
    right, left = lax.rem(gx + 1, n_gx), lax.rem(gx + n_gx - 1, n_gx)
    modes = v_ref.shape[0]
    fields = c_ref.shape[0]
    part = modes // n_gx
    sub = part // chunks
    pairs = n_ma // 2
    twin = ma + 1 - 2 * lax.rem(ma, 2)
    greet(gx, n_gx, ma, n_ma)

    size = modes // pieces
    far = {}
    for p in range(pieces):
        for d in range(1, pairs):
            far[p, d] = remote(
                v_ref.at[pl.ds(p * size, size)],
                all_ref.at[pl.ds(ma * modes + p * size, size)],
                s_p.at[p, d], r_p.at[p, d], "ma", lax.rem(ma + 2 * d, n_ma),
            )
    side = [
        remote(c_ref, side_ref.at[1], s_c.at[1], r_c.at[1], "gx", right),
        remote(c_ref, side_ref.at[0], s_c.at[0], r_c.at[0], "gx", left),
    ]
    near = [remote(v_ref, all_ref.at[pl.ds(ma * modes, modes)], s_o.at[0], r_o.at[0], "ma", twin)]
    means = [
        remote(c_ref.at[0], mean_ref.at[gx], s_m.at[d], r_m.at[d], "gx", lax.rem(gx + d, n_gx))
        for d in range(1, n_gx)
    ]
    all_ref[pl.ds(ma * modes, modes)] = v_ref[...]
    mean_ref[gx] = c_ref[0]
    for k in range(fields):
        for m, face in enumerate(faces_of(c_ref[k])):
            f_ref[m, k] = face
    for p in range(pieces):
        for d in range(1, pairs):
            far[p, d].wait()
            rows = pl.ds(lax.rem(ma + n_ma - 2 * d, n_ma) * modes + p * size, size)
            near.append(
                remote(all_ref.at[rows], all_ref.at[rows], s_f.at[p, d], r_f.at[p, d], "ma", twin)
            )
        if p == 0:
            for copy in side:
                copy.wait()
            for k in range(fields):
                f_ref[4, k] = 0.5 * (c_ref[k] + side_ref[0, k])
                f_ref[5, k] = 0.5 * (c_ref[k] + side_ref[1, k])
            for copy in means:
                copy.wait()
            for s in range(n_gx):
                c = mean_ref[s]
                f = faces_of(c) + [
                    0.5 * (c + mean_ref[(s + 1) % n_gx]),
                    0.5 * (c + mean_ref[(s + n_gx - 1) % n_gx]),
                ]
                for m in range(6):
                    fm_ref[m, s] = f[m]
                fm_ref[6, s] = f[0] + f[1] + f[2] + f[3] + f[4] + f[5] + 1.0
    for copy in near:
        copy.wait()

    halos = []
    for q in range(chunks):

        def body(d, carry):
            base = d * part + q * sub
            values = [v_ref[base + g] for g in range(sub)]
            f = [f_ref[m, 0] for m in range(6)]
            sums = [[f[m] * values[g] for m in range(6)] for g in range(sub)]
            for k in range(1, fields):
                row = 2 * (k - 1)
                f = [f_ref[m, k] for m in range(6)]
                for g in range(sub):
                    i = base + g
                    h = wt_ref[row, i] * all_ref[part_ref[row, i]] + wt_ref[row + 1, i] * all_ref[part_ref[row + 1, i]]
                    sums[g] = [sums[g][m] + f[m] * h for m in range(6)]
            for g in range(sub):
                t = sums[g]
                image = values[g] + (t[0] + t[1] + t[2] + t[3] + t[4] + t[5]) - shift_faces(t)
                u_ref[q, d, g] = src_ref[base + g] - image
                qr_ref[q, d, g] = t[4]
                ql_ref[q, d, g] = t[5]
            return carry

        lax.fori_loop(0, n_gx, body, 0)
        halos.append(
            (
                remote(qr_ref.at[q], from_left.at[q], s_h.at[q, 0], r_h.at[q, 0], "gx", right),
                remote(ql_ref.at[q], from_right.at[q], s_h.at[q, 1], r_h.at[q, 1], "gx", left),
            )
        )

    moved = {}
    returned = []

    def settle(q):
        for copy in halos[q]:
            copy.wait()
        cols = pl.ds(q * sub, sub)
        for d in range(n_gx):
            res_ref[d, cols] = u_ref[q, d] + from_left[q, d] + from_right[q, d]
        moved[q] = [
            remote(
                res_ref.at[lax.rem(gx + d, n_gx), cols], trans.at[q, gx],
                s_t.at[q, d], r_t.at[q, d], "gx", lax.rem(gx + d, n_gx),
            )
            for d in range(1, n_gx)
        ]
        trans[q, gx] = res_ref[gx, cols]

    def polish(q):
        for copy in moved[q]:
            copy.wait()
        theta = 13.0
        delta = 12.0
        sigma = theta / delta

        def one(mode, carry):
            remain = [trans[q, s, mode] for s in range(n_gx)]
            direction = [r * (1.0 / theta) for r in remain]
            total = direction
            rho = 1.0 / sigma
            for _ in range(STEPS):
                rho_next = 1.0 / (2.0 * sigma - rho)
                ny, nz = direction[0].shape
                fresh = []
                for s in range(n_gx):
                    v = direction[s]
                    applied = (
                        fm_ref[6, s] * v
                        - fm_ref[0, s] * pltpu.roll(v, ny - 1, 0)
                        - fm_ref[1, s] * pltpu.roll(v, 1, 0)
                        - fm_ref[2, s] * pltpu.roll(v, nz - 1, 1)
                        - fm_ref[3, s] * pltpu.roll(v, 1, 1)
                        - fm_ref[4, s] * direction[(s + 1) % n_gx]
                        - fm_ref[5, s] * direction[(s + n_gx - 1) % n_gx]
                    )
                    fresh.append(remain[s] - applied)
                remain = fresh
                direction = [
                    (rho_next * rho) * direction[s] + (2.0 * rho_next / delta) * remain[s] for s in range(n_gx)
                ]
                total = [total[s] + direction[s] for s in range(n_gx)]
                rho = rho_next
            for s in range(n_gx):
                back[q, s, mode] = total[s]
            return carry

        lax.fori_loop(0, sub, one, 0)
        cols = pl.ds(q * sub, sub)
        for d in range(1, n_gx):
            target = lax.rem(gx + d, n_gx)
            returned.append(
                remote(back.at[q, target], cor_ref.at[gx, cols], s_b.at[q, d], r_b.at[q, d], "gx", target)
            )
        cor_ref[gx, cols] = back[q, gx]

    settle(0)
    for q in range(chunks):
        if q + 1 < chunks:
            settle(q + 1)
        polish(q)
    for copy in returned:
        copy.wait()


def shards(n_gx, n_ma, solution, source, mean_conductivity, kl_fields, couplings, mode_index):
    modes = solution.shape[0]
    shape = solution.shape
    ny, nz = shape[2], shape[3]
    fields = kl_fields.shape[0]
    start = lax.axis_index("ma") * modes
    f32 = jnp.float32
    here = lax.dynamic_slice_in_dim(couplings, start, modes, 1)
    degree = lax.dynamic_slice_in_dim(mode_index, start, modes, 0).T.astype(f32)
    ids = start + lax.broadcasted_iota(jnp.int32, (1, modes, 1), 1)
    strength = jnp.sqrt(jnp.stack([degree + 1.0, degree], -1))
    weight = jnp.where(here != ids, strength, 0.0)
    partner = here.transpose(0, 2, 1).reshape(2 * fields, modes)
    weight = weight.transpose(0, 2, 1).reshape(2 * fields, modes)
    stacked = jnp.concatenate([mean_conductivity, kl_fields[:, 0]], 0)
    v = solution.reshape(modes, ny, nz)
    src = source.reshape(modes, ny, nz)
    part = modes // n_gx
    chunks = next(n for n in (4, 2, 1) if part % n == 0)
    pieces = next(n for n in (4, 2, 1) if modes % n == 0)
    sub = part // chunks
    pairs = n_ma // 2
    dma = pltpu.SemaphoreType.DMA
    vmem = lambda *lead: pltpu.VMEM(lead + (ny, nz), f32)
    field = jax.ShapeDtypeStruct((n_gx, part, ny, nz), f32)
    residual, correction = pl.pallas_call(
        functools.partial(kernel, n_gx, n_ma, chunks, pieces),
        out_shape=(field,) * 2,
        in_specs=[SMEM] * 2 + [VMEM] * 3,
        out_specs=(VMEM,) * 2,
        scratch_shapes=[
            vmem(n_ma * modes),
            vmem(2, fields + 1),
            vmem(n_gx),
            vmem(6, fields + 1),
            vmem(7, n_gx),
        ]
        + [vmem(chunks, n_gx, sub)] * 7
        + [dma((pieces, pairs))] * 4
        + [dma((1,))] * 2
        + [dma((2,))] * 2
        + [dma((n_gx,))] * 2
        + [dma((chunks, 2))] * 2
        + [dma((chunks, n_gx))] * 4,
        compiler_params=pltpu.CompilerParams(collective_id=0, has_side_effects=True, vmem_limit_bytes=LIMIT),
    )(partner, weight, v, src, stacked)
    return residual.reshape(shape), correction.reshape(shape)


def solution(mesh):
    in_specs = (
        P("ma", "gx", None, None),
        P("ma", "gx", None, None),
        P("gx", None, None),
        P(None, "gx", None, None),
        P(),
        P(),
    )
    out_specs = (P("ma", "gx", None, None), P("ma", "gx", None, None))
    body = functools.partial(shards, mesh.shape["gx"], mesh.shape["ma"])
    return jax.shard_map(body, mesh=mesh, in_specs=in_specs, out_specs=out_specs, check_vma=False)
```

```python
import functools

import jax
import jax.numpy as jnp
from jax import lax
from jax.experimental import pallas as pl
from jax.experimental.pallas import tpu as pltpu
from jax.sharding import PartitionSpec as P

STEPS = 3
MESH = pl.DeviceIdType.MESH
VMEM = pl.BlockSpec(memory_space=pltpu.VMEM)
SMEM = pl.BlockSpec(memory_space=pltpu.SMEM)
HBM = pl.BlockSpec(memory_space=pltpu.HBM)
LIMIT = 40 * 1024 * 1024


def greet(gx, n_gx, ma, n_ma):
    barrier = pltpu.get_barrier_semaphore()
    for d in range(1, n_gx):
        pl.semaphore_signal(barrier, inc=1, device_id={"gx": lax.rem(gx + d, n_gx)}, device_id_type=MESH)
    for d in range(1, n_ma):
        pl.semaphore_signal(barrier, inc=1, device_id={"ma": lax.rem(ma + d, n_ma)}, device_id_type=MESH)
    pl.semaphore_wait(barrier, max(n_gx - 1, 0) + max(n_ma - 1, 0))


def remote(src, dst, send, recv, axis, index):
    copy = pltpu.make_async_remote_copy(
        src_ref=src, dst_ref=dst, send_sem=send, recv_sem=recv, device_id={axis: index}, device_id_type=MESH
    )
    copy.start()
    return copy


def faces_of(c):
    ny, nz = c.shape[-2], c.shape[-1]
    return [
        0.5 * (c + pltpu.roll(c, ny - 1, c.ndim - 2)),
        0.5 * (c + pltpu.roll(c, 1, c.ndim - 2)),
        0.5 * (c + pltpu.roll(c, nz - 1, c.ndim - 1)),
        0.5 * (c + pltpu.roll(c, 1, c.ndim - 1)),
    ]


def shift_faces(q):
    ny, nz = q[0].shape[-2], q[0].shape[-1]
    d = q[0].ndim
    return (
        pltpu.roll(q[1], ny - 1, d - 2)
        + pltpu.roll(q[0], 1, d - 2)
        + pltpu.roll(q[3], nz - 1, d - 1)
        + pltpu.roll(q[2], 1, d - 1)
    )


def kernel(
    n_gx, n_ma, chunks, pieces, halves, part_ref, wt_ref, v_hbm, src_hbm, c0_ref, c_ref, res_ref, cor_ref,
    all_refs, v_ref, src_ref, side_ref, mean_ref, f_ref, fm_ref, u_ref, qr_refs, ql_refs, from_left, from_right, trans, back,
    s_p, r_p, s_f, r_f, s_o, r_o, s_c, r_c, s_m, r_m, s_h, r_h, s_t, r_t, s_b, r_b, s_in,
):
    gx, ma = lax.axis_index("gx"), lax.axis_index("ma")
    right, left = lax.rem(gx + 1, n_gx), lax.rem(gx + n_gx - 1, n_gx)
    modes = v_ref.shape[0]
    fields = c_ref.shape[0] + 1
    half = v_ref.shape[-1] // halves
    part = modes // n_gx
    sub = part // chunks
    pairs = n_ma // 2
    twin = ma + 1 - 2 * lax.rem(ma, 2)
    inputs = [
        pltpu.make_async_copy(v_hbm, v_ref, s_in.at[0]),
        pltpu.make_async_copy(src_hbm, src_ref, s_in.at[1]),
    ]
    for copy in inputs:
        copy.start()
    greet(gx, n_gx, ma, n_ma)
    mine = pl.ds(ma * modes, modes)
    lanes = [pl.ds(h * half, half) for h in range(halves)]
    joined = lambda parts: jnp.concatenate(parts, -1) if len(parts) > 1 else parts[0]

    size = modes // pieces
    far, near = {}, {}
    means = [
        remote(c0_ref.at[0], mean_ref.at[gx], s_m.at[d], r_m.at[d], "gx", lax.rem(gx + d, n_gx))
        for d in range(1, n_gx)
    ]
    side = [
        remote(c_ref, side_ref.at[1], s_c.at[1], r_c.at[1], "gx", right),
        remote(c_ref, side_ref.at[0], s_c.at[0], r_c.at[0], "gx", left),
    ]
    for h in range(halves):
        for p in range(pieces):
            for d in range(1, pairs):
                far[h, p, d] = remote(
                    v_hbm.at[pl.ds(p * size, size), :, lanes[h]],
                    all_refs[h].at[pl.ds(ma * modes + p * size, size)],
                    s_p.at[h, p, d], r_p.at[h, p, d], "ma", lax.rem(ma + 2 * d, n_ma),
                )
    for h in range(halves):
        near[h] = [remote(v_hbm.at[:, :, lanes[h]], all_refs[h].at[mine], s_o.at[h], r_o.at[h], "ma", twin)]
    mean_ref[gx] = c0_ref[0]
    for k in range(1, fields):
        for m, face in enumerate(faces_of(c_ref[k - 1])):
            f_ref[m, k] = face
    inputs[0].wait()
    for h in range(halves):
        all_refs[h][mine] = v_ref[:, :, h * half : (h + 1) * half]
    for copy in means:
        copy.wait()
    for s in range(n_gx):
        c = mean_ref[s]
        f = faces_of(c) + [
            0.5 * (c + mean_ref[(s + 1) % n_gx]),
            0.5 * (c + mean_ref[(s + n_gx - 1) % n_gx]),
        ]
        for m in range(6):
            fm_ref[m, s] = f[m]
        fm_ref[6, s] = f[0] + f[1] + f[2] + f[3] + f[4] + f[5] + 1.0
    for m in range(6):
        f_ref[m, 0] = fm_ref[m, gx]
    for copy in side:
        copy.wait()
    for k in range(1, fields):
        f_ref[4, k] = 0.5 * (c_ref[k - 1] + side_ref[0, k - 1])
        f_ref[5, k] = 0.5 * (c_ref[k - 1] + side_ref[1, k - 1])
    inputs[1].wait()

    halos = {}

    def exchange(q, h):
        halos[q, h] = (
            remote(qr_refs[h].at[q], from_left[h].at[q], s_h.at[h, q, 0], r_h.at[h, q, 0], "gx", right),
            remote(ql_refs[h].at[q], from_right[h].at[q], s_h.at[h, q, 1], r_h.at[h, q, 1], "gx", left),
        )

    for h in range(halves):
        for p in range(pieces):
            for d in range(1, pairs):
                far[h, p, d].wait()
                rows = pl.ds(lax.rem(ma + n_ma - 2 * d, n_ma) * modes + p * size, size)
                near[h].append(
                    remote(all_refs[h].at[rows], all_refs[h].at[rows], s_f.at[h, p, d], r_f.at[h, p, d], "ma", twin)
                )
        for copy in near[h]:
            copy.wait()
        if h + 1 == halves:
            break
        for q in range(chunks):

            def ahead(d, carry):
                base = d * part + q * sub
                cut = slice(h * half, (h + 1) * half)
                f = [f_ref[m, 0, :, cut] for m in (4, 5)]
                sums = [[x * v_ref[base + g, :, cut] for x in f] for g in range(sub)]
                for k in range(1, fields):
                    row = 2 * (k - 1)
                    f = [f_ref[m, k, :, cut] for m in (4, 5)]
                    for g in range(sub):
                        i = base + g
                        value = (
                            wt_ref[row, i] * all_refs[h][part_ref[row, i]]
                            + wt_ref[row + 1, i] * all_refs[h][part_ref[row + 1, i]]
                        )
                        sums[g] = [total + x * value for total, x in zip(sums[g], f)]
                for g in range(sub):
                    qr_refs[h][q, d, g] = sums[g][0]
                    ql_refs[h][q, d, g] = sums[g][1]
                return carry

            lax.fori_loop(0, n_gx, ahead, 0)
            exchange(q, h)

    for q in range(chunks):

        def body(d, carry):
            base = d * part + q * sub
            values = [v_ref[base + g] for g in range(sub)]
            f = [f_ref[m, 0] for m in range(6)]
            sums = [[f[m] * values[g] for m in range(6)] for g in range(sub)]
            for k in range(1, fields):
                row = 2 * (k - 1)
                f = [f_ref[m, k] for m in range(6)]
                for g in range(sub):
                    i = base + g
                    h = joined(
                        [
                            wt_ref[row, i] * ref[part_ref[row, i]] + wt_ref[row + 1, i] * ref[part_ref[row + 1, i]]
                            for ref in all_refs
                        ]
                    )
                    sums[g] = [sums[g][m] + f[m] * h for m in range(6)]
            for g in range(sub):
                t = sums[g]
                image = values[g] + (t[0] + t[1] + t[2] + t[3] + t[4] + t[5]) - shift_faces(t)
                u_ref[q, d, g] = src_ref[base + g] - image
                qr_refs[-1][q, d, g] = t[4][:, (halves - 1) * half :]
                ql_refs[-1][q, d, g] = t[5][:, (halves - 1) * half :]
            return carry

        lax.fori_loop(0, n_gx, body, 0)
        exchange(q, halves - 1)

    moved = {}
    returned = []

    def settle(q):
        for h in range(halves):
            for copy in halos[q, h]:
                copy.wait()
        cols = pl.ds(q * sub, sub)
        for d in range(n_gx):
            res_ref[d, cols] = u_ref[q, d] + joined([a[q, d] + b[q, d] for a, b in zip(from_left, from_right)])
        moved[q] = [
            remote(
                res_ref.at[lax.rem(gx + d, n_gx), cols], trans.at[q, gx],
                s_t.at[q, d], r_t.at[q, d], "gx", lax.rem(gx + d, n_gx),
            )
            for d in range(1, n_gx)
        ]
        trans[q, gx] = res_ref[gx, cols]

    def polish(q):
        for copy in moved[q]:
            copy.wait()
        theta = 13.0
        delta = 12.0
        sigma = theta / delta

        def one(mode, carry):
            remain = [trans[q, s, mode] for s in range(n_gx)]
            direction = [r * (1.0 / theta) for r in remain]
            total = direction
            rho = 1.0 / sigma
            for _ in range(STEPS):
                rho_next = 1.0 / (2.0 * sigma - rho)
                ny, nz = direction[0].shape
                fresh = []
                for s in range(n_gx):
                    v = direction[s]
                    applied = (
                        fm_ref[6, s] * v
                        - fm_ref[0, s] * pltpu.roll(v, ny - 1, 0)
                        - fm_ref[1, s] * pltpu.roll(v, 1, 0)
                        - fm_ref[2, s] * pltpu.roll(v, nz - 1, 1)
                        - fm_ref[3, s] * pltpu.roll(v, 1, 1)
                        - fm_ref[4, s] * direction[(s + 1) % n_gx]
                        - fm_ref[5, s] * direction[(s + n_gx - 1) % n_gx]
                    )
                    fresh.append(remain[s] - applied)
                remain = fresh
                direction = [
                    (rho_next * rho) * direction[s] + (2.0 * rho_next / delta) * remain[s] for s in range(n_gx)
                ]
                total = [total[s] + direction[s] for s in range(n_gx)]
                rho = rho_next
            for s in range(n_gx):
                back[q, s, mode] = total[s]
            return carry

        lax.fori_loop(0, sub, one, 0)
        cols = pl.ds(q * sub, sub)
        for d in range(1, n_gx):
            target = lax.rem(gx + d, n_gx)
            returned.append(
                remote(back.at[q, target], cor_ref.at[gx, cols], s_b.at[q, d], r_b.at[q, d], "gx", target)
            )
        cor_ref[gx, cols] = back[q, gx]

    settle(0)
    for q in range(chunks):
        if q + 1 < chunks:
            settle(q + 1)
        polish(q)
    for copy in returned:
        copy.wait()


def shards(n_gx, n_ma, solution, source, mean_conductivity, kl_fields, couplings, mode_index):
    modes = solution.shape[0]
    shape = solution.shape
    ny, nz = shape[2], shape[3]
    fields = kl_fields.shape[0]
    start = lax.axis_index("ma") * modes
    f32 = jnp.float32
    here = lax.dynamic_slice_in_dim(couplings, start, modes, 1)
    degree = lax.dynamic_slice_in_dim(mode_index, start, modes, 0).T.astype(f32)
    ids = start + lax.broadcasted_iota(jnp.int32, (1, modes, 1), 1)
    strength = jnp.sqrt(jnp.stack([degree + 1.0, degree], -1))
    weight = jnp.where(here != ids, strength, 0.0)
    partner = here.transpose(0, 2, 1).reshape(2 * fields, modes)
    weight = weight.transpose(0, 2, 1).reshape(2 * fields, modes)
    halves = 2 if nz % 256 == 0 else 1
    v = solution.reshape(modes, ny, nz)
    src = source.reshape(modes, ny, nz)
    part = modes // n_gx
    chunks = next(n for n in (4, 2, 1) if part % n == 0)
    pieces = next(n for n in (2, 1) if modes % n == 0)
    sub = part // chunks
    pairs = n_ma // 2
    dma = pltpu.SemaphoreType.DMA
    vmem = lambda *lead: pltpu.VMEM(lead + (ny, nz), f32)
    split = lambda *lead: (pltpu.VMEM(lead + (ny, nz // halves), f32),) * halves
    field = jax.ShapeDtypeStruct((n_gx, part, ny, nz), f32)
    residual, correction = pl.pallas_call(
        functools.partial(kernel, n_gx, n_ma, chunks, pieces, halves),
        out_shape=(field,) * 2,
        in_specs=[SMEM] * 2 + [HBM] * 2 + [VMEM] * 2,
        out_specs=(VMEM,) * 2,
        scratch_shapes=[
            split(n_ma * modes),
            vmem(modes),
            vmem(modes),
            vmem(2, fields),
            vmem(n_gx),
            vmem(6, fields + 1),
            vmem(7, n_gx),
            vmem(chunks, n_gx, sub),
        ]
        + [split(chunks, n_gx, sub)] * 4
        + [vmem(chunks, n_gx, sub)] * 2
        + [dma((halves, pieces, pairs))] * 4
        + [dma((halves,))] * 2
        + [dma((2,))] * 2
        + [dma((n_gx,))] * 2
        + [dma((halves, chunks, 2))] * 2
        + [dma((chunks, n_gx))] * 4
        + [dma((2,))],
        compiler_params=pltpu.CompilerParams(collective_id=0, has_side_effects=True, vmem_limit_bytes=LIMIT),
    )(partner, weight, v, src, mean_conductivity, kl_fields.reshape(fields, ny, nz))
    return residual.reshape(shape), correction.reshape(shape)


def solution(mesh):
    in_specs = (
        P("ma", "gx", None, None),
        P("ma", "gx", None, None),
        P("gx", None, None),
        P(None, "gx", None, None),
        P(),
        P(),
    )
    out_specs = (P("ma", "gx", None, None), P("ma", "gx", None, None))
    body = functools.partial(shards, mesh.shape["gx"], mesh.shape["ma"])
    return jax.shard_map(body, mesh=mesh, in_specs=in_specs, out_specs=out_specs, check_vma=False)
```

```python
import functools

import jax
import jax.numpy as jnp
from jax import lax
from jax.experimental import pallas as pl
from jax.experimental.pallas import tpu as pltpu
from jax.sharding import PartitionSpec as P

STEPS = 3
MESH = pl.DeviceIdType.MESH
VMEM = pl.BlockSpec(memory_space=pltpu.VMEM)
SMEM = pl.BlockSpec(memory_space=pltpu.SMEM)
HBM = pl.BlockSpec(memory_space=pltpu.HBM)
LIMIT = 40 * 1024 * 1024


def greet(gx, n_gx, ma, n_ma):
    barrier = pltpu.get_barrier_semaphore()
    for d in range(1, n_gx):
        pl.semaphore_signal(barrier, inc=1, device_id={"gx": lax.rem(gx + d, n_gx)}, device_id_type=MESH)
    for d in range(1, n_ma):
        pl.semaphore_signal(barrier, inc=1, device_id={"ma": lax.rem(ma + d, n_ma)}, device_id_type=MESH)
    pl.semaphore_wait(barrier, max(n_gx - 1, 0) + max(n_ma - 1, 0))


def remote(src, dst, send, recv, axis, index):
    copy = pltpu.make_async_remote_copy(
        src_ref=src, dst_ref=dst, send_sem=send, recv_sem=recv, device_id={axis: index}, device_id_type=MESH
    )
    copy.start()
    return copy


def faces_of(c):
    ny, nz = c.shape[-2], c.shape[-1]
    return [
        0.5 * (c + pltpu.roll(c, ny - 1, c.ndim - 2)),
        0.5 * (c + pltpu.roll(c, 1, c.ndim - 2)),
        0.5 * (c + pltpu.roll(c, nz - 1, c.ndim - 1)),
        0.5 * (c + pltpu.roll(c, 1, c.ndim - 1)),
    ]


def shift_faces(q):
    ny, nz = q[0].shape[-2], q[0].shape[-1]
    d = q[0].ndim
    return (
        pltpu.roll(q[1], ny - 1, d - 2)
        + pltpu.roll(q[0], 1, d - 2)
        + pltpu.roll(q[3], nz - 1, d - 1)
        + pltpu.roll(q[2], 1, d - 1)
    )


def kernel(
    n_gx, n_ma, chunks, pieces, halves, part_ref, wt_ref, v_hbm, src_hbm, c0_ref, c_ref, res_ref, cor_ref,
    all_refs, v_ref, src_ref, side_ref, mean_ref, f_ref, fm_ref, u_ref, qr_refs, ql_refs, from_left, from_right, trans, back,
    s_p, r_p, s_f, r_f, s_o, r_o, s_c, r_c, s_m, r_m, s_h, r_h, s_t, r_t, s_b, r_b, s_in,
):
    gx, ma = lax.axis_index("gx"), lax.axis_index("ma")
    right, left = lax.rem(gx + 1, n_gx), lax.rem(gx + n_gx - 1, n_gx)
    modes = v_ref.shape[0]
    fields = c_ref.shape[0] + 1
    half = v_ref.shape[-1] // halves
    part = modes // n_gx
    sub = part // chunks
    pairs = n_ma // 2
    twin = ma + 1 - 2 * lax.rem(ma, 2)
    inputs = [
        pltpu.make_async_copy(v_hbm, v_ref, s_in.at[0]),
        pltpu.make_async_copy(src_hbm, src_ref, s_in.at[1]),
    ]
    for copy in inputs:
        copy.start()
    greet(gx, n_gx, ma, n_ma)
    mine = pl.ds(ma * modes, modes)
    lanes = [pl.ds(h * half, half) for h in range(halves)]
    joined = lambda parts: jnp.concatenate(parts, -1) if len(parts) > 1 else parts[0]

    size = modes // pieces
    far, near = {}, {}
    means = [
        remote(c0_ref.at[0], mean_ref.at[gx], s_m.at[d], r_m.at[d], "gx", lax.rem(gx + d, n_gx))
        for d in range(1, n_gx)
    ]
    side = [
        remote(c_ref, side_ref.at[1], s_c.at[1], r_c.at[1], "gx", right),
        remote(c_ref, side_ref.at[0], s_c.at[0], r_c.at[0], "gx", left),
    ]
    for h in range(halves):
        for p in range(pieces):
            for d in range(1, pairs):
                far[h, p, d] = remote(
                    v_hbm.at[pl.ds(p * size, size), :, lanes[h]],
                    all_refs[h].at[pl.ds(ma * modes + p * size, size)],
                    s_p.at[h, p, d], r_p.at[h, p, d], "ma", lax.rem(ma + 2 * d, n_ma),
                )
    for h in range(halves):
        near[h] = [remote(v_hbm.at[:, :, lanes[h]], all_refs[h].at[mine], s_o.at[h], r_o.at[h], "ma", twin)]
    mean_ref[gx] = c0_ref[0]
    for k in range(1, fields):
        for m, face in enumerate(faces_of(c_ref[k - 1])):
            f_ref[m, k] = face
    inputs[0].wait()
    for h in range(halves):
        all_refs[h][mine] = v_ref[:, :, h * half : (h + 1) * half]
    for copy in means:
        copy.wait()
    for s in range(n_gx):
        c = mean_ref[s]
        f = faces_of(c) + [
            0.5 * (c + mean_ref[(s + 1) % n_gx]),
            0.5 * (c + mean_ref[(s + n_gx - 1) % n_gx]),
        ]
        for m in range(6):
            fm_ref[m, s] = f[m]
        fm_ref[6, s] = f[0] + f[1] + f[2] + f[3] + f[4] + f[5] + 1.0
    for m in range(6):
        f_ref[m, 0] = fm_ref[m, gx]
    for copy in side:
        copy.wait()
    for k in range(1, fields):
        f_ref[4, k] = 0.5 * (c_ref[k - 1] + side_ref[0, k - 1])
        f_ref[5, k] = 0.5 * (c_ref[k - 1] + side_ref[1, k - 1])
    inputs[1].wait()

    halos = {}

    def exchange(q, h):
        halos[q, h] = (
            remote(qr_refs[h].at[q], from_left[h].at[q], s_h.at[h, q, 0], r_h.at[h, q, 0], "gx", right),
            remote(ql_refs[h].at[q], from_right[h].at[q], s_h.at[h, q, 1], r_h.at[h, q, 1], "gx", left),
        )

    for h in range(halves):
        for p in range(pieces):
            for d in range(1, pairs):
                far[h, p, d].wait()
                rows = pl.ds(lax.rem(ma + n_ma - 2 * d, n_ma) * modes + p * size, size)
                near[h].append(
                    remote(all_refs[h].at[rows], all_refs[h].at[rows], s_f.at[h, p, d], r_f.at[h, p, d], "ma", twin)
                )
        for copy in near[h]:
            copy.wait()
        if h + 1 == halves:
            break
        for q in range(chunks):

            def ahead(d, carry):
                base = d * part + q * sub
                cut = slice(h * half, (h + 1) * half)
                f = [f_ref[m, 0, :, cut] for m in (4, 5)]
                sums = [[x * v_ref[base + g, :, cut] for x in f] for g in range(sub)]
                for k in range(1, fields):
                    row = 2 * (k - 1)
                    f = [f_ref[m, k, :, cut] for m in (4, 5)]
                    for g in range(sub):
                        i = base + g
                        value = (
                            wt_ref[row, i] * all_refs[h][part_ref[row, i]]
                            + wt_ref[row + 1, i] * all_refs[h][part_ref[row + 1, i]]
                        )
                        sums[g] = [total + x * value for total, x in zip(sums[g], f)]
                for g in range(sub):
                    qr_refs[h][q, d, g] = sums[g][0]
                    ql_refs[h][q, d, g] = sums[g][1]
                return carry

            lax.fori_loop(0, n_gx, ahead, 0)
            exchange(q, h)

    for q in range(chunks):

        def body(d, carry):
            base = d * part + q * sub
            values = [v_ref[base + g] for g in range(sub)]
            f = [f_ref[m, 0] for m in range(6)]
            sums = [[f[m] * values[g] for m in range(6)] for g in range(sub)]
            for k in range(1, fields):
                row = 2 * (k - 1)
                f = [f_ref[m, k] for m in range(6)]
                for g in range(sub):
                    i = base + g
                    h = joined(
                        [
                            wt_ref[row, i] * ref[part_ref[row, i]] + wt_ref[row + 1, i] * ref[part_ref[row + 1, i]]
                            for ref in all_refs
                        ]
                    )
                    sums[g] = [sums[g][m] + f[m] * h for m in range(6)]
            for g in range(sub):
                t = sums[g]
                image = values[g] + (t[0] + t[1] + t[2] + t[3] + t[4] + t[5]) - shift_faces(t)
                u_ref[q, d, g] = src_ref[base + g] - image
                qr_refs[-1][q, d, g] = t[4][:, (halves - 1) * half :]
                ql_refs[-1][q, d, g] = t[5][:, (halves - 1) * half :]
            return carry

        lax.fori_loop(0, n_gx, body, 0)
        exchange(q, halves - 1)

    moved = {}
    returned = []

    def settle(q):
        for h in range(halves):
            for copy in halos[q, h]:
                copy.wait()
        cols = pl.ds(q * sub, sub)
        for d in range(n_gx):
            res_ref[d, cols] = u_ref[q, d] + joined([a[q, d] + b[q, d] for a, b in zip(from_left, from_right)])
        moved[q] = [
            remote(
                res_ref.at[lax.rem(gx + d, n_gx), cols], trans.at[q, gx],
                s_t.at[q, d], r_t.at[q, d], "gx", lax.rem(gx + d, n_gx),
            )
            for d in range(1, n_gx)
        ]
        trans[q, gx] = res_ref[gx, cols]

    def polish(q):
        for copy in moved[q]:
            copy.wait()
        theta = 13.0
        delta = 12.0
        sigma = theta / delta

        def one(mode, carry):
            remain = [trans[q, s, mode] for s in range(n_gx)]
            direction = [r * (1.0 / theta) for r in remain]
            total = direction
            rho = 1.0 / sigma
            for _ in range(STEPS):
                rho_next = 1.0 / (2.0 * sigma - rho)
                ny, nz = direction[0].shape
                fresh = []
                for s in range(n_gx):
                    v = direction[s]
                    applied = (
                        fm_ref[6, s] * v
                        - fm_ref[0, s] * pltpu.roll(v, ny - 1, 0)
                        - fm_ref[1, s] * pltpu.roll(v, 1, 0)
                        - fm_ref[2, s] * pltpu.roll(v, nz - 1, 1)
                        - fm_ref[3, s] * pltpu.roll(v, 1, 1)
                        - fm_ref[4, s] * direction[(s + 1) % n_gx]
                        - fm_ref[5, s] * direction[(s + n_gx - 1) % n_gx]
                    )
                    fresh.append(remain[s] - applied)
                remain = fresh
                direction = [
                    (rho_next * rho) * direction[s] + (2.0 * rho_next / delta) * remain[s] for s in range(n_gx)
                ]
                total = [total[s] + direction[s] for s in range(n_gx)]
                rho = rho_next
            for s in range(n_gx):
                back[q, s, mode] = total[s]
            return carry

        lax.fori_loop(0, sub, one, 0)
        cols = pl.ds(q * sub, sub)
        for d in range(1, n_gx):
            target = lax.rem(gx + d, n_gx)
            returned.append(
                remote(back.at[q, target], cor_ref.at[gx, cols], s_b.at[q, d], r_b.at[q, d], "gx", target)
            )
        cor_ref[gx, cols] = back[q, gx]

    for q in range(chunks):
        settle(q)
    for q in range(chunks):
        polish(q)
    for copy in returned:
        copy.wait()


def shards(n_gx, n_ma, solution, source, mean_conductivity, kl_fields, couplings, mode_index):
    modes = solution.shape[0]
    shape = solution.shape
    ny, nz = shape[2], shape[3]
    fields = kl_fields.shape[0]
    start = lax.axis_index("ma") * modes
    f32 = jnp.float32
    here = lax.dynamic_slice_in_dim(couplings, start, modes, 1)
    degree = lax.dynamic_slice_in_dim(mode_index, start, modes, 0).T.astype(f32)
    ids = start + lax.broadcasted_iota(jnp.int32, (1, modes, 1), 1)
    strength = jnp.sqrt(jnp.stack([degree + 1.0, degree], -1))
    weight = jnp.where(here != ids, strength, 0.0)
    partner = here.transpose(0, 2, 1).reshape(2 * fields, modes)
    weight = weight.transpose(0, 2, 1).reshape(2 * fields, modes)
    halves = 2 if nz % 256 == 0 else 1
    v = solution.reshape(modes, ny, nz)
    src = source.reshape(modes, ny, nz)
    part = modes // n_gx
    chunks = next(n for n in (4, 2, 1) if part % n == 0)
    pieces = next(n for n in (2, 1) if modes % n == 0)
    sub = part // chunks
    pairs = n_ma // 2
    dma = pltpu.SemaphoreType.DMA
    vmem = lambda *lead: pltpu.VMEM(lead + (ny, nz), f32)
    split = lambda *lead: (pltpu.VMEM(lead + (ny, nz // halves), f32),) * halves
    field = jax.ShapeDtypeStruct((n_gx, part, ny, nz), f32)
    residual, correction = pl.pallas_call(
        functools.partial(kernel, n_gx, n_ma, chunks, pieces, halves),
        out_shape=(field,) * 2,
        in_specs=[SMEM] * 2 + [HBM] * 2 + [VMEM] * 2,
        out_specs=(VMEM,) * 2,
        scratch_shapes=[
            split(n_ma * modes),
            vmem(modes),
            vmem(modes),
            vmem(2, fields),
            vmem(n_gx),
            vmem(6, fields + 1),
            vmem(7, n_gx),
            vmem(chunks, n_gx, sub),
        ]
        + [split(chunks, n_gx, sub)] * 4
        + [vmem(chunks, n_gx, sub)] * 2
        + [dma((halves, pieces, pairs))] * 4
        + [dma((halves,))] * 2
        + [dma((2,))] * 2
        + [dma((n_gx,))] * 2
        + [dma((halves, chunks, 2))] * 2
        + [dma((chunks, n_gx))] * 4
        + [dma((2,))],
        compiler_params=pltpu.CompilerParams(collective_id=0, has_side_effects=True, vmem_limit_bytes=LIMIT),
    )(partner, weight, v, src, mean_conductivity, kl_fields.reshape(fields, ny, nz))
    return residual.reshape(shape), correction.reshape(shape)


def solution(mesh):
    in_specs = (
        P("ma", "gx", None, None),
        P("ma", "gx", None, None),
        P("gx", None, None),
        P(None, "gx", None, None),
        P(),
        P(),
    )
    out_specs = (P("ma", "gx", None, None), P("ma", "gx", None, None))
    body = functools.partial(shards, mesh.shape["gx"], mesh.shape["ma"])
    return jax.shard_map(body, mesh=mesh, in_specs=in_specs, out_specs=out_specs, check_vma=False)
```

```python
import functools

import jax
import jax.numpy as jnp
from jax import lax
from jax.experimental import pallas as pl
from jax.experimental.pallas import tpu as pltpu
from jax.sharding import PartitionSpec as P

STEPS = 3
MESH = pl.DeviceIdType.MESH
VMEM = pl.BlockSpec(memory_space=pltpu.VMEM)
SMEM = pl.BlockSpec(memory_space=pltpu.SMEM)
HBM = pl.BlockSpec(memory_space=pltpu.HBM)
LIMIT = 40 * 1024 * 1024


def greet(gx, n_gx, ma, n_ma):
    barrier = pltpu.get_barrier_semaphore()
    for d in range(1, n_gx):
        pl.semaphore_signal(barrier, inc=1, device_id={"gx": lax.rem(gx + d, n_gx)}, device_id_type=MESH)
    for d in range(1, n_ma):
        pl.semaphore_signal(barrier, inc=1, device_id={"ma": lax.rem(ma + d, n_ma)}, device_id_type=MESH)
    pl.semaphore_wait(barrier, max(n_gx - 1, 0) + max(n_ma - 1, 0))


def remote(src, dst, send, recv, axis, index):
    copy = pltpu.make_async_remote_copy(
        src_ref=src, dst_ref=dst, send_sem=send, recv_sem=recv, device_id={axis: index}, device_id_type=MESH
    )
    copy.start()
    return copy


def faces_of(c):
    ny, nz = c.shape[-2], c.shape[-1]
    return [
        0.5 * (c + pltpu.roll(c, ny - 1, c.ndim - 2)),
        0.5 * (c + pltpu.roll(c, 1, c.ndim - 2)),
        0.5 * (c + pltpu.roll(c, nz - 1, c.ndim - 1)),
        0.5 * (c + pltpu.roll(c, 1, c.ndim - 1)),
    ]


def shift_faces(q):
    ny, nz = q[0].shape[-2], q[0].shape[-1]
    d = q[0].ndim
    return (
        pltpu.roll(q[1], ny - 1, d - 2)
        + pltpu.roll(q[0], 1, d - 2)
        + pltpu.roll(q[3], nz - 1, d - 1)
        + pltpu.roll(q[2], 1, d - 1)
    )


def kernel(
    n_gx, n_ma, chunks, pieces, halves, part_ref, wt_ref, v_hbm, src_hbm, c0_ref, c_ref, res_ref, cor_ref,
    all_refs, v_ref, src_ref, side_ref, mean_ref, f_ref, fm_ref, u_ref, qr_refs, ql_refs, from_left, from_right, trans, back,
    s_p, r_p, s_f, r_f, s_o, r_o, s_c, r_c, s_m, r_m, s_h, r_h, s_t, r_t, s_b, r_b, s_in,
):
    gx, ma = lax.axis_index("gx"), lax.axis_index("ma")
    right, left = lax.rem(gx + 1, n_gx), lax.rem(gx + n_gx - 1, n_gx)
    modes = v_ref.shape[0]
    fields = c_ref.shape[0] + 1
    half = v_ref.shape[-1] // halves
    part = modes // n_gx
    sub = part // chunks
    pairs = n_ma // 2
    twin = ma + 1 - 2 * lax.rem(ma, 2)
    inputs = [
        pltpu.make_async_copy(v_hbm, v_ref, s_in.at[0]),
        pltpu.make_async_copy(src_hbm, src_ref, s_in.at[1]),
    ]
    for copy in inputs:
        copy.start()
    greet(gx, n_gx, ma, n_ma)
    mine = pl.ds(ma * modes, modes)
    lanes = [pl.ds(h * half, half) for h in range(halves)]
    joined = lambda parts: jnp.concatenate(parts, -1) if len(parts) > 1 else parts[0]

    size = modes // pieces
    far, near = {}, {}
    means = [
        remote(c0_ref.at[0], mean_ref.at[gx], s_m.at[d], r_m.at[d], "gx", lax.rem(gx + d, n_gx))
        for d in range(1, n_gx)
    ]
    side = [
        remote(c_ref, side_ref.at[1], s_c.at[1], r_c.at[1], "gx", right),
        remote(c_ref, side_ref.at[0], s_c.at[0], r_c.at[0], "gx", left),
    ]
    def send(h):
        for p in range(pieces):
            for d in range(1, pairs):
                far[h, p, d] = remote(
                    v_hbm.at[pl.ds(p * size, size), :, lanes[h]],
                    all_refs[h].at[pl.ds(ma * modes + p * size, size)],
                    s_p.at[h, p, d], r_p.at[h, p, d], "ma", lax.rem(ma + 2 * d, n_ma),
                )
        near[h] = [remote(v_hbm.at[:, :, lanes[h]], all_refs[h].at[mine], s_o.at[h], r_o.at[h], "ma", twin)]

    send(0)
    mean_ref[gx] = c0_ref[0]
    for k in range(1, fields):
        for m, face in enumerate(faces_of(c_ref[k - 1])):
            f_ref[m, k] = face
    inputs[0].wait()
    for h in range(halves):
        all_refs[h][mine] = v_ref[:, :, h * half : (h + 1) * half]
    for copy in means:
        copy.wait()
    for s in range(n_gx):
        c = mean_ref[s]
        f = faces_of(c) + [
            0.5 * (c + mean_ref[(s + 1) % n_gx]),
            0.5 * (c + mean_ref[(s + n_gx - 1) % n_gx]),
        ]
        for m in range(6):
            fm_ref[m, s] = f[m]
        fm_ref[6, s] = f[0] + f[1] + f[2] + f[3] + f[4] + f[5] + 1.0
    for m in range(6):
        f_ref[m, 0] = fm_ref[m, gx]
    for copy in side:
        copy.wait()
    for k in range(1, fields):
        f_ref[4, k] = 0.5 * (c_ref[k - 1] + side_ref[0, k - 1])
        f_ref[5, k] = 0.5 * (c_ref[k - 1] + side_ref[1, k - 1])
    inputs[1].wait()

    halos = {}

    def exchange(q, h):
        halos[q, h] = (
            remote(qr_refs[h].at[q], from_left[h].at[q], s_h.at[h, q, 0], r_h.at[h, q, 0], "gx", right),
            remote(ql_refs[h].at[q], from_right[h].at[q], s_h.at[h, q, 1], r_h.at[h, q, 1], "gx", left),
        )

    for h in range(halves):
        for p in range(pieces):
            for d in range(1, pairs):
                far[h, p, d].wait()
                rows = pl.ds(lax.rem(ma + n_ma - 2 * d, n_ma) * modes + p * size, size)
                near[h].append(
                    remote(all_refs[h].at[rows], all_refs[h].at[rows], s_f.at[h, p, d], r_f.at[h, p, d], "ma", twin)
                )
        if h + 1 < halves:
            send(h + 1)
        for copy in near[h]:
            copy.wait()
        if h + 1 == halves:
            break
        for q in range(chunks):

            def ahead(d, carry):
                base = d * part + q * sub
                cut = slice(h * half, (h + 1) * half)
                f = [f_ref[m, 0, :, cut] for m in (4, 5)]
                sums = [[x * v_ref[base + g, :, cut] for x in f] for g in range(sub)]
                for k in range(1, fields):
                    row = 2 * (k - 1)
                    f = [f_ref[m, k, :, cut] for m in (4, 5)]
                    for g in range(sub):
                        i = base + g
                        value = (
                            wt_ref[row, i] * all_refs[h][part_ref[row, i]]
                            + wt_ref[row + 1, i] * all_refs[h][part_ref[row + 1, i]]
                        )
                        sums[g] = [total + x * value for total, x in zip(sums[g], f)]
                for g in range(sub):
                    qr_refs[h][q, d, g] = sums[g][0]
                    ql_refs[h][q, d, g] = sums[g][1]
                return carry

            lax.fori_loop(0, n_gx, ahead, 0)
            exchange(q, h)

    for q in range(chunks):

        def body(d, carry):
            base = d * part + q * sub
            values = [v_ref[base + g] for g in range(sub)]
            f = [f_ref[m, 0] for m in range(6)]
            sums = [[f[m] * values[g] for m in range(6)] for g in range(sub)]
            for k in range(1, fields):
                row = 2 * (k - 1)
                f = [f_ref[m, k] for m in range(6)]
                for g in range(sub):
                    i = base + g
                    h = joined(
                        [
                            wt_ref[row, i] * ref[part_ref[row, i]] + wt_ref[row + 1, i] * ref[part_ref[row + 1, i]]
                            for ref in all_refs
                        ]
                    )
                    sums[g] = [sums[g][m] + f[m] * h for m in range(6)]
            for g in range(sub):
                t = sums[g]
                image = values[g] + (t[0] + t[1] + t[2] + t[3] + t[4] + t[5]) - shift_faces(t)
                u_ref[q, d, g] = src_ref[base + g] - image
                qr_refs[-1][q, d, g] = t[4][:, (halves - 1) * half :]
                ql_refs[-1][q, d, g] = t[5][:, (halves - 1) * half :]
            return carry

        lax.fori_loop(0, n_gx, body, 0)
        exchange(q, halves - 1)

    moved = {}
    returned = []

    def settle(q):
        for h in range(halves):
            for copy in halos[q, h]:
                copy.wait()
        cols = pl.ds(q * sub, sub)
        for d in range(n_gx):
            res_ref[d, cols] = u_ref[q, d] + joined([a[q, d] + b[q, d] for a, b in zip(from_left, from_right)])
        moved[q] = [
            remote(
                res_ref.at[lax.rem(gx + d, n_gx), cols], trans.at[q, gx],
                s_t.at[q, d], r_t.at[q, d], "gx", lax.rem(gx + d, n_gx),
            )
            for d in range(1, n_gx)
        ]
        trans[q, gx] = res_ref[gx, cols]

    def polish(q):
        for copy in moved[q]:
            copy.wait()
        theta = 13.0
        delta = 12.0
        sigma = theta / delta

        def one(mode, carry):
            remain = [trans[q, s, mode] for s in range(n_gx)]
            direction = [r * (1.0 / theta) for r in remain]
            total = direction
            rho = 1.0 / sigma
            for _ in range(STEPS):
                rho_next = 1.0 / (2.0 * sigma - rho)
                ny, nz = direction[0].shape
                fresh = []
                for s in range(n_gx):
                    v = direction[s]
                    applied = (
                        fm_ref[6, s] * v
                        - fm_ref[0, s] * pltpu.roll(v, ny - 1, 0)
                        - fm_ref[1, s] * pltpu.roll(v, 1, 0)
                        - fm_ref[2, s] * pltpu.roll(v, nz - 1, 1)
                        - fm_ref[3, s] * pltpu.roll(v, 1, 1)
                        - fm_ref[4, s] * direction[(s + 1) % n_gx]
                        - fm_ref[5, s] * direction[(s + n_gx - 1) % n_gx]
                    )
                    fresh.append(remain[s] - applied)
                remain = fresh
                direction = [
                    (rho_next * rho) * direction[s] + (2.0 * rho_next / delta) * remain[s] for s in range(n_gx)
                ]
                total = [total[s] + direction[s] for s in range(n_gx)]
                rho = rho_next
            for s in range(n_gx):
                back[q, s, mode] = total[s]
            return carry

        lax.fori_loop(0, sub, one, 0)
        cols = pl.ds(q * sub, sub)
        for d in range(1, n_gx):
            target = lax.rem(gx + d, n_gx)
            returned.append(
                remote(back.at[q, target], cor_ref.at[gx, cols], s_b.at[q, d], r_b.at[q, d], "gx", target)
            )
        cor_ref[gx, cols] = back[q, gx]

    for q in range(chunks):
        settle(q)
    for q in range(chunks):
        polish(q)
    for copy in returned:
        copy.wait()


def shards(n_gx, n_ma, solution, source, mean_conductivity, kl_fields, couplings, mode_index):
    modes = solution.shape[0]
    shape = solution.shape
    ny, nz = shape[2], shape[3]
    fields = kl_fields.shape[0]
    start = lax.axis_index("ma") * modes
    f32 = jnp.float32
    here = lax.dynamic_slice_in_dim(couplings, start, modes, 1)
    degree = lax.dynamic_slice_in_dim(mode_index, start, modes, 0).T.astype(f32)
    ids = start + lax.broadcasted_iota(jnp.int32, (1, modes, 1), 1)
    strength = jnp.sqrt(jnp.stack([degree + 1.0, degree], -1))
    weight = jnp.where(here != ids, strength, 0.0)
    partner = here.transpose(0, 2, 1).reshape(2 * fields, modes)
    weight = weight.transpose(0, 2, 1).reshape(2 * fields, modes)
    halves = 2 if nz % 256 == 0 else 1
    v = solution.reshape(modes, ny, nz)
    src = source.reshape(modes, ny, nz)
    part = modes // n_gx
    chunks = next(n for n in (4, 2, 1) if part % n == 0)
    pieces = next(n for n in (2, 1) if modes % n == 0)
    sub = part // chunks
    pairs = n_ma // 2
    dma = pltpu.SemaphoreType.DMA
    vmem = lambda *lead: pltpu.VMEM(lead + (ny, nz), f32)
    split = lambda *lead: (pltpu.VMEM(lead + (ny, nz // halves), f32),) * halves
    field = jax.ShapeDtypeStruct((n_gx, part, ny, nz), f32)
    residual, correction = pl.pallas_call(
        functools.partial(kernel, n_gx, n_ma, chunks, pieces, halves),
        out_shape=(field,) * 2,
        in_specs=[SMEM] * 2 + [HBM] * 2 + [VMEM] * 2,
        out_specs=(VMEM,) * 2,
        scratch_shapes=[
            split(n_ma * modes),
            vmem(modes),
            vmem(modes),
            vmem(2, fields),
            vmem(n_gx),
            vmem(6, fields + 1),
            vmem(7, n_gx),
            vmem(chunks, n_gx, sub),
        ]
        + [split(chunks, n_gx, sub)] * 4
        + [vmem(chunks, n_gx, sub)] * 2
        + [dma((halves, pieces, pairs))] * 4
        + [dma((halves,))] * 2
        + [dma((2,))] * 2
        + [dma((n_gx,))] * 2
        + [dma((halves, chunks, 2))] * 2
        + [dma((chunks, n_gx))] * 4
        + [dma((2,))],
        compiler_params=pltpu.CompilerParams(collective_id=0, has_side_effects=True, vmem_limit_bytes=LIMIT),
    )(partner, weight, v, src, mean_conductivity, kl_fields.reshape(fields, ny, nz))
    return residual.reshape(shape), correction.reshape(shape)


def solution(mesh):
    in_specs = (
        P("ma", "gx", None, None),
        P("ma", "gx", None, None),
        P("gx", None, None),
        P(None, "gx", None, None),
        P(),
        P(),
    )
    out_specs = (P("ma", "gx", None, None), P("ma", "gx", None, None))
    body = functools.partial(shards, mesh.shape["gx"], mesh.shape["ma"])
    return jax.shard_map(body, mesh=mesh, in_specs=in_specs, out_specs=out_specs, check_vma=False)
```
